32 devices in a mesh: batch: 4 (over z), pos: 8 (over y, x, core).
Axes of the slice: x: 2, y: 2, z: 4, core: 2. Of those that a mesh axis runs over, the one named last changes fastest.
Arguments:
- inputs: bfloat16 [4, 4096, 1536], P('batch', 'pos'), may hold values from -6 to 6
- bn_scale: float32 [1536], replicated, may hold values from 0.25 to 1.75
- bn_shift: float32 [1536], replicated, may hold values from -2 to 2
- mid_scale: float32 [384], replicated, may hold values from 0.25 to 1.75
- mid_shift: float32 [384], replicated, may hold values from -2 to 2
- dilated_weight: bfloat16 [1536, 3, 384], P('batch'), may hold values from -0.09375 to 0.09375
- w_point: bfloat16 [384, 1536], P('batch'), may hold values from -0.3125 to 0.3125
- head: bfloat16 [5120, 1536], P('pos'), may hold values from -0.15625 to 0.15625
- targets: bfloat16 [4, 4096, 512], P('batch', 'pos'), may hold values from 0 to 2
- assay_slots: int32 [4, 512], P('batch', 'pos'), may hold values from 0 to 639, as said below
- assay_counts: int32 [4, 8], P('batch', 'pos'), may hold values from 1 to 64, as said below
Outputs:
- d_inputs: bfloat16 [4, 4096, 1536], P('batch', 'pos')
- new_head: bfloat16 [5120, 1536], P('pos')
The draws below stay inside these ranges and needn't reach their ends.
Inputs may be any that keep to these rules, and one draw needn't show every extreme that they name: `assay_slots`: within each block of 64 slots (one shard of one sequence) the entries are distinct. `assay_counts`: in every sequence some shard has all 64 slots live.
All inputs are finite; a program needn't handle non-finite values.
Results may differ from the reference program's by a relative error of at most 0.012.
Values may be sent and summed in bfloat16 or wider, within the bound.
A program may use at most 64 MiB of HBM per device.

```python
import jax
import jax.numpy as jnp
from jax import lax

STREAM_CHANNELS = 1536
HIDDEN_CHANNELS = 384
DILATION_STEP = 32
TRACKS = 5120
ASSAY = 512
BIN_DEV = 512
SEQS = 4
SEQUENCE_BINS = 4096
SHARDS = 8
TRK_DEV = 640
ASLOT = 64
N_POS = 8


def draw_assay_slots(key, part):
    scores = jax.random.randint(key, (SEQS, SHARDS, TRK_DEV), 0, 1 << 20) * TRK_DEV + jnp.arange(TRK_DEV).astype(jnp.int32)
    order = jnp.argsort(scores, axis=-1)
    return order[:, :, :ASLOT].reshape(SEQS, ASSAY).astype(jnp.int32)


def draw_assay_counts(key, part):
    first_key, second_key = jax.random.split(key)
    base = jax.random.randint(first_key, (SEQS, SHARDS), 1, ASLOT + 1)
    full = jax.random.randint(second_key, (SEQS, 1), 0, SHARDS)
    marks = jnp.arange(SHARDS).astype(jnp.int32)[None, :] == full
    return jnp.where(marks, ASLOT, base).astype(jnp.int32)


def steps_of(own_key, shape, cuts, least, largest):
    level = 1.0
    for axis_at, shards_of in cuts:
        steps = jax.random.uniform(jax.random.fold_in(jax.random.fold_in(own_key, 6), axis_at), (shards_of,), jnp.float32, least / len(cuts), largest / len(cuts))
        level = level * jnp.repeat(jnp.exp(steps), shape[axis_at] // shards_of).reshape((-1,) + (1,) * (len(shape) - 1 - axis_at))
    return level


def bell_draw(rng, shape, scale, most, cuts=(), dtype=jnp.bfloat16):
    entries = jax.random.normal(rng, shape, jnp.float32) * scale
    if len(cuts) > 0:
        entries = steps_of(rng, shape, cuts, -0.22, 0.18) * entries
    return jnp.clip(entries, min=-most, max=most).astype(dtype)


def setup_inputs(seed: int = 0) -> dict:
    keys = jax.random.split(jax.random.key(seed), 12)
    return {
        "inputs": bell_draw(keys[0], (SEQS, SEQUENCE_BINS, STREAM_CHANNELS), 1.0, 6.0, ((0, 4), (1, 8))),
        "bn_scale": jnp.clip(1.0 + 0.15 * jax.random.normal(keys[1], (STREAM_CHANNELS,), jnp.float32), 0.25, 1.75),
        "bn_shift": bell_draw(keys[2], (STREAM_CHANNELS,), 0.4, 2.0, (), jnp.float32),
        "mid_scale": jnp.clip(1.0 + 0.15 * jax.random.normal(keys[3], (HIDDEN_CHANNELS,), jnp.float32), 0.25, 1.75),
        "mid_shift": bell_draw(keys[4], (HIDDEN_CHANNELS,), 0.4, 2.0, (), jnp.float32),
        "dilated_weight": bell_draw(keys[5], (STREAM_CHANNELS, 3, HIDDEN_CHANNELS), (3 * STREAM_CHANNELS) ** -0.5, 0.09375, ((0, 4),)),
        "w_point": bell_draw(keys[6], (HIDDEN_CHANNELS, STREAM_CHANNELS), HIDDEN_CHANNELS ** -0.5, 0.3125, ((0, 4),)),
        "head": bell_draw(keys[7], (TRACKS, STREAM_CHANNELS), STREAM_CHANNELS ** -0.5, 0.15625, ((0, 8),)),
        "targets": jnp.clip(2.0 * jax.random.uniform(keys[8], (SEQS, SEQUENCE_BINS, ASSAY), jnp.float32) ** steps_of(keys[8], (SEQS, SEQUENCE_BINS, ASSAY), ((0, 4), (1, 8)), -0.2, 0.2), 0.0, 2.0).astype(jnp.bfloat16),
        "assay_slots": draw_assay_slots(jax.random.fold_in(keys[11], 71), 0),
        "assay_counts": draw_assay_counts(jax.random.fold_in(keys[11], 71), 0),
    }


def gelu_slope(value):
    return jax.jvp(jax.nn.gelu, (value,), (jnp.ones_like(value),))[1]


def reference(inputs, bn_scale, bn_shift, mid_scale, mid_shift, dilated_weight, w_point, head, targets, assay_slots, assay_counts):
    slot_ids = jnp.arange(ASSAY).astype(jnp.int32)
    shard_ids = (slot_ids // ASLOT).astype(jnp.int32)
    within = (slot_ids - shard_ids * ASLOT).astype(jnp.int32)
    contract = (((1,), (1,)), ((), ()))

    def one_sequence(total, item):
        seq, goal, slots, counts = item
        rows = (shard_ids * TRK_DEV + slots).astype(jnp.int32)
        live = (within < counts[shard_ids]).astype(jnp.float32)
        selected = head[rows]
        first = seq.astype(jnp.float32) * bn_scale + bn_shift
        acted = jax.nn.gelu(first).astype(jnp.bfloat16)
        border_bins = jnp.zeros((DILATION_STEP, STREAM_CHANNELS), jnp.bfloat16)
        padded_input = jnp.concatenate([border_bins, acted, border_bins], axis=0)
        hidden_state = jnp.zeros((SEQUENCE_BINS, HIDDEN_CHANNELS), jnp.float32)
        for kernel_offset in range(3):
            hidden_state = hidden_state + jnp.dot(padded_input[kernel_offset * DILATION_STEP:kernel_offset * DILATION_STEP + SEQUENCE_BINS], dilated_weight[:, kernel_offset, :], preferred_element_type=jnp.float32)
        second = hidden_state * mid_scale + mid_shift
        mid = jax.nn.gelu(second).astype(jnp.bfloat16)
        embed = (seq.astype(jnp.float32) + jnp.dot(mid, w_point, preferred_element_type=jnp.float32)).astype(jnp.bfloat16)
        pre = lax.dot_general(embed, selected, contract, preferred_element_type=jnp.float32)
        delta = (live * (jax.nn.softplus(pre) - goal.astype(jnp.float32)) * jax.nn.sigmoid(pre)).astype(jnp.bfloat16)
        back = jnp.dot(delta, selected, preferred_element_type=jnp.float32).astype(jnp.bfloat16)
        dmid = lax.dot_general(back, w_point, contract, preferred_element_type=jnp.float32)
        dhid = (dmid * gelu_slope(second) * mid_scale).astype(jnp.bfloat16)
        hidden_border = jnp.zeros((DILATION_STEP, HIDDEN_CHANNELS), jnp.bfloat16)
        padded_h = jnp.concatenate([hidden_border, dhid, hidden_border], axis=0)
        dact = jnp.zeros((SEQUENCE_BINS, STREAM_CHANNELS), jnp.float32)
        for kernel_offset in range(3):
            start_offset = (2 - kernel_offset) * DILATION_STEP
            dact = dact + lax.dot_general(padded_h[start_offset:start_offset + SEQUENCE_BINS], dilated_weight[:, kernel_offset, :], contract, preferred_element_type=jnp.float32)
        d_in = (back.astype(jnp.float32) + dact * gelu_slope(first) * bn_scale).astype(jnp.bfloat16)
        parts = jnp.einsum("pba,pbc->pac", delta.reshape(N_POS, BIN_DEV, ASSAY).astype(jnp.float32), embed.reshape(N_POS, BIN_DEV, STREAM_CHANNELS).astype(jnp.float32))
        parts = lax.optimization_barrier(parts.astype(jnp.bfloat16)).astype(jnp.float32)
        grads = jnp.sum(parts, axis=0)
        total = total.at[rows].add(grads)
        return total, d_in

    total, d_inputs = lax.scan(one_sequence, jnp.zeros((TRACKS, STREAM_CHANNELS), jnp.float32), (inputs, targets, assay_slots, assay_counts))
    new_head = (head.astype(jnp.float32) - 0.004 * total).astype(jnp.bfloat16)
    return (d_inputs, new_head)
```

```python
import functools

import jax
import jax.numpy as jnp
from jax import lax
from jax.experimental import pallas as pl
from jax.experimental.pallas import tpu as pltpu
from jax.sharding import PartitionSpec as P

STEP = 32
MESH = pl.DeviceIdType.MESH
F32 = jnp.float32
BF16 = jnp.bfloat16
ROOT = 0.7978845608028654
CUBE = 0.044715


def gelu(v):
    return 0.5 * v * (1.0 + jnp.tanh(ROOT * (v + CUBE * v * v * v)))


def gelu_slope(v):
    sq = v * v
    t = jnp.tanh(ROOT * (v + CUBE * v * sq))
    return 0.5 * (1.0 + t) + 0.5 * v * (1.0 - t * t) * (ROOT * (1.0 + 3.0 * CUBE * sq))


def dot(a, b):
    return jnp.dot(a, b, preferred_element_type=F32)


def dot_t(a, b):
    return lax.dot_general(a, b, (((1,), (1,)), ((), ())), preferred_element_type=F32)


def tdot(a, b):
    return lax.dot_general(a, b, (((0,), (0,)), ((), ())), preferred_element_type=F32)


def kernel(nb, npos, spread, *refs):
    refs = list(refs)
    take = lambda n: [refs.pop(0) for _ in range(n)]
    x, bsc, bsh, msc, msh, packed = take(6)
    if not spread:
        (wp,) = take(1)
    head, goal, meta = take(3)
    d_in, new_head = take(2)
    if spread:
        w, wp = take(2)
    else:
        w = packed
    acted, hidden, mid, embed, sel, delta, back, dpad, xh = take(9)
    grads, r1buf, part, r2buf, rows_all, meta_all, onehot = take(7)
    (halo_s, halo_r, meta_s, meta_r, sel_s, sel_r, self_s, self_r, r1_s, r1_r, r2_s, r2_r, r3_s, r3_r) = take(14)
    if spread:
        own_sem, w1_s, w1_r, w2_s, w2_r, wf_s, wf_r = take(7)

    z = lax.axis_index("batch")
    p = lax.axis_index("pos")
    chip, core = p // 2, p % 2
    nchip = npos // 2
    sib = chip * 2 + (1 - core)
    nrows, width = x.shape
    nz = w.shape[0]
    cw = width // nz
    hid = mid.shape[1]
    nslot = delta.shape[1]
    aslot = sel.shape[1]

    def rc(src, dst, s, r, zz, pp):
        return pltpu.make_async_remote_copy(
            src_ref=src, dst_ref=dst, send_sem=s, recv_sem=r, device_id=(zz, pp), device_id_type=MESH
        )

    def at_chip(d):
        return lax.rem(chip + d, nchip)

    def from_chip(d):
        return lax.rem(chip - d + nchip, nchip)

    bar = pltpu.get_barrier_semaphore()
    for d in range(1, npos):
        pl.semaphore_signal(bar, inc=1, device_id=(z, lax.rem(p + d, npos)), device_id_type=MESH)
    for d in range(1, nb):
        pl.semaphore_signal(bar, inc=1, device_id=(lax.rem(z + d, nb), p), device_id_type=MESH)
    pl.semaphore_wait(bar, npos - 1 + nb - 1)

    sends = []

    def go(c):
        c.start()
        sends.append(c)

    right, left = lax.rem(p + 1, npos), lax.rem(p + npos - 1, npos)

    def chain(src, dst, ss, rr):
        def copy(di, k, first):
            zz = z - k if di == 0 else z + k
            to = z + 1 if di == 0 else z - 1
            return rc(src if first else dst(zz), dst(zz), ss.at[di, k], rr.at[di, k], to, p)

        def can_send(di, k):
            if di == 0:
                return jnp.logical_and(z + 1 < nb, z - k >= 0)
            return jnp.logical_and(z - 1 >= 0, z + k < nb)

        def start(di, k):
            @pl.when(can_send(di, k))
            def _():
                copy(di, k, k == 0).start()

        def arrive(di, k, body):
            has = (z - k - 1 >= 0) if di == 0 else (z + k + 1 < nb)

            @pl.when(has)
            def _():
                zz = z - k - 1 if di == 0 else z + k + 1
                rc(dst(zz), dst(zz), ss.at[di, k], rr.at[di, k], z, sib).wait_recv()

            if k + 1 < nb - 1:
                start(di, k + 1)
            if body is not None:
                @pl.when(has)
                def _():
                    body(z - k - 1 if di == 0 else z + k + 1)

        def finish():
            for di in (0, 1):
                for k in range(nb - 1):
                    @pl.when(can_send(di, k))
                    def _():
                        copy(di, k, k == 0).wait_send()

        return start, arrive, finish

    if spread:
        w_start, w_arrive, w_finish = chain(packed.at[p], lambda zz: w.at[zz, p], w1_s, w1_r)
        w_start(0, 0)
        w_start(1, 0)
    go(rc(x.at[pl.ds(0, STEP)], xh.at[1], halo_s.at[0], halo_r.at[1], z, left))
    go(rc(x.at[pl.ds(nrows - STEP, STEP)], xh.at[0], halo_s.at[1], halo_r.at[0], z, right))
    for d in range(1, nb):
        go(rc(meta, meta_all.at[z], meta_s.at[d], meta_r.at[d], lax.rem(z + d, nb), p))
    if spread:
        own = pltpu.make_async_copy(packed, w.at[z], own_sem)
        own.start()

    ntrk = head.shape[0]

    def marks(m):
        return (m[:, 0:1] == lax.broadcasted_iota(jnp.int32, (aslot, ntrk), 1)).astype(BF16)

    sel[p] = dot(marks(meta[...]), head[...]).astype(BF16)
    for d in range(1, nchip):
        go(rc(sel.at[p], sel.at[p], sel_s.at[d], sel_r.at[d], z, at_chip(d) * 2 + core))
    go(rc(sel.at[p], sel.at[p], self_s.at[0], self_r.at[0], z, sib))

    def act_chunk(i):
        cols = pl.ds(i * cw, cw)
        first = x[:, cols].astype(F32) * bsc[:, cols] + bsh[:, cols]
        acted[i, STEP : STEP + nrows] = gelu(first).astype(BF16)

    def w_spread(di, k):
        def body(zz):
            for d in range(1, nchip):
                rc(w.at[zz, p], w.at[zz, p], w2_s.at[di, k, d], w2_r.at[di, k, d], z, at_chip(d) * 2 + core).start()
            rc(w.at[zz, p], w.at[zz, p], wf_s.at[di, k, 0], wf_r.at[di, k, 0], z, sib).start()

        w_arrive(di, k, body)

    def w_shard(di, k):
        zz = z - k - 1 if di == 0 else z + k + 1
        has = (zz >= 0) if di == 0 else (zz < nb)
        return zz, has

    def w_forward(di, k):
        zz, has = w_shard(di, k)

        @pl.when(has)
        def _():
            for d in range(1, nchip):
                q = from_chip(d) * 2 + core
                rc(w.at[zz, q], w.at[zz, q], w2_s.at[di, k, d], w2_r.at[di, k, d], z, sib).wait_recv()
                rc(w.at[zz, q], w.at[zz, q], wf_s.at[di, k, d], wf_r.at[di, k, d], z, sib).start()

    def w_ready(di, k):
        zz, has = w_shard(di, k)

        @pl.when(has)
        def _():
            for d in range(nchip):
                q = from_chip(d) * 2 + 1 - core
                rc(w.at[zz, q], w.at[zz, q], wf_s.at[di, k, d], wf_r.at[di, k, d], z, sib).wait_recv()
            conv(zz)

    def w_done(di, k):
        zz, has = w_shard(di, k)

        @pl.when(has)
        def _():
            for d in range(1, nchip):
                rc(w.at[zz, p], w.at[zz, p], w2_s.at[di, k, d], w2_r.at[di, k, d], z, sib).wait_send()
            for d in range(nchip):
                rc(w.at[zz, p], w.at[zz, p], wf_s.at[di, k, d], wf_r.at[di, k, d], z, sib).wait_send()

    def wrows(zz, lo, n):
        return w[zz, :, :, lo : lo + n].reshape(cw, n)

    def conv(zz):
        total = hidden[...]
        for k in range(3):
            total = total + dot(acted[zz, k * STEP : k * STEP + nrows], wrows(zz, k * hid, hid))
        hidden[...] = total

    def sel_forward():
        for d in range(1, nchip):
            q = from_chip(d) * 2 + core
            rc(sel.at[q], sel.at[q], sel_s.at[d], sel_r.at[d], z, sib).wait_recv()
            go(rc(sel.at[q], sel.at[q], self_s.at[d], self_r.at[d], z, sib))

    steps = range(nb - 1) if spread else range(0)
    hidden[...] = jnp.zeros_like(hidden)
    for i in range(nz):
        act_chunk(i)
        if i == 0:
            for k in steps[:1]:
                w_spread(0, k)
                w_spread(1, k)
        if i == 1:
            sel_forward()
            for k in steps[1:2]:
                w_spread(0, k)
                w_spread(1, k)
    for side, edge in ((0, 0), (1, npos - 1)):
        rc(xh.at[side], xh.at[side], halo_s.at[side], halo_r.at[side], z, sib).wait_recv()
        keep = jnp.where(p == edge, 0.0, 1.0)
        for i in range(nz):
            cols = pl.ds(i * cw, cw)
            first = xh[side, :, cols].astype(F32) * bsc[:, cols] + bsh[:, cols]
            lo = 0 if side == 0 else STEP + nrows
            acted[i, lo : lo + STEP] = (gelu(first) * keep).astype(BF16)
    if spread:
        for k in steps[2:]:
            w_forward(0, k - 2)
            w_forward(1, k - 2)
            w_spread(0, k)
            w_spread(1, k)
        own.wait()
        conv(z)
        for k in steps[max(0, len(steps) - 2) :]:
            w_forward(0, k)
            w_forward(1, k)
        for k in steps:
            w_ready(0, k)
            w_ready(1, k)
        rest = width // hid
        per = npos // rest
        for zz in range(nb):
            for q in range(rest):
                blk = w[zz, q * per : (q + 1) * per, :, 3 * hid : 4 * hid].reshape(cw // rest, hid)
                wp[zz * (cw // rest) : (zz + 1) * (cw // rest), q * hid : (q + 1) * hid] = blk
    else:
        for i in range(nz):
            conv(i)

    second = hidden[...] * msc[...] + msh[...]
    mid[...] = gelu(second).astype(BF16)
    half = 512
    for n in range(0, width, half):
        embed[:, n : n + half] = (x[:, n : n + half].astype(F32) + dot(mid[...], wp[:, n : n + half])).astype(BF16)

    for d in range(nchip):
        q = from_chip(d) * 2 + 1 - core
        rc(sel.at[q], sel.at[q], self_s.at[d], self_r.at[d], z, sib).wait_recv()

    group = 256
    per_group = group // aslot
    for j in range(0, nslot, group):
        s = sel[j // aslot : j // aslot + per_group].reshape(group, width)
        pre = dot_t(embed[...], s)
        e = jnp.exp(-jnp.abs(pre))
        soft = jnp.maximum(pre, 0.0) + jnp.log1p(e)
        sig = jnp.where(pre >= 0.0, 1.0, e) / (1.0 + e)
        delta[:, j : j + group] = ((soft - goal[:, j : j + group].astype(F32)) * sig).astype(BF16)
        for n in range(0, width, half):
            g = tdot(delta[:, j : j + group], embed[:, n : n + half]).astype(BF16)
            grads[j // aslot : j // aslot + per_group, :, n : n + half] = g.reshape(per_group, aslot, half)

    order = list(range(1, nchip)) + [0]
    for d in order:
        go(rc(grads.at[at_chip(d) * 2 + 1 - core], r1buf.at[d], r1_s.at[d], r1_r.at[d], z, sib))

    for n in range(0, width, half):
        back[:, n : n + half] = dot(delta[...], sel[:, :, n : n + half].reshape(nslot, half)).astype(BF16)

    for d in order:
        rc(r1buf.at[d], r1buf.at[d], r1_s.at[d], r1_r.at[d], z, sib).wait_recv()
        part[d] = (grads[at_chip(d) * 2 + core].astype(F32) + r1buf[d].astype(F32)).astype(BF16)
        if d:
            go(rc(part.at[d], r2buf.at[d], r2_s.at[d], r2_r.at[d], z, at_chip(d) * 2 + core))

    dmid = dot_t(back[...], wp[...])
    second = hidden[...] * msc[...] + msh[...]
    dpad[STEP : STEP + nrows] = (dmid * gelu_slope(second) * msc[...]).astype(BF16)
    go(rc(dpad.at[pl.ds(STEP, STEP)], dpad.at[pl.ds(STEP + nrows, STEP)], halo_s.at[2], halo_r.at[3], z, left))
    go(rc(dpad.at[pl.ds(nrows, STEP)], dpad.at[pl.ds(0, STEP)], halo_s.at[3], halo_r.at[2], z, right))

    total = part[0].astype(F32)
    for d in range(1, nchip):
        rc(r2buf.at[d], r2buf.at[d], r2_s.at[d], r2_r.at[d], z, sib).wait_recv()
        total = total + r2buf[d].astype(F32)
    rows_all[z] = total.astype(BF16)
    g_start, g_arrive, g_finish = chain(rows_all.at[z], lambda zz: rows_all.at[zz], r3_s, r3_r)
    g_start(0, 0)
    g_start(1, 0)

    for side, edge, lo in ((0, 0, 0), (1, npos - 1, STEP + nrows)):
        rc(dpad.at[pl.ds(lo, STEP)], dpad.at[pl.ds(lo, STEP)], halo_s.at[2], halo_r.at[2 + side], z, sib).wait_recv()

        @pl.when(p == edge)
        def _():
            dpad[lo : lo + STEP] = jnp.zeros((STEP, hid), BF16)

    arrivals = list(range(nb - 1))
    for i in range(nz):
        cols = pl.ds(i * cw, cw)
        dact = dot_t(dpad[2 * STEP : 2 * STEP + nrows], wrows(i, 0, hid))
        dact = dact + dot_t(dpad[STEP : STEP + nrows], wrows(i, hid, hid))
        dact = dact + dot_t(dpad[0:nrows], wrows(i, 2 * hid, hid))
        first = x[:, cols].astype(F32) * bsc[:, cols] + bsh[:, cols]
        d_in[:, cols] = (back[:, cols].astype(F32) + dact * gelu_slope(first) * bsc[:, cols]).astype(BF16)
        if i < nz - 1 and arrivals:
            k = arrivals.pop(0)
            g_arrive(0, k, None)
            g_arrive(1, k, None)
    for k in arrivals:
        g_arrive(0, k, None)
        g_arrive(1, k, None)

    for d in range(1, nb):
        zz = lax.rem(z - d + nb, nb)
        rc(meta_all.at[zz], meta_all.at[zz], meta_s.at[d], meta_r.at[d], z, sib).wait_recv()
    meta_all[z] = meta[...]
    for zz in range(nb):
        onehot[zz * aslot : (zz + 1) * aslot] = marks(meta_all[zz])
    for n in range(0, width, half):
        d_head = tdot(onehot[...], rows_all[:, :, n : n + half].reshape(nb * aslot, half))
        new_head[:, n : n + half] = (head[:, n : n + half].astype(F32) - 0.004 * d_head).astype(BF16)

    for c in sends:
        c.wait_send()
    g_finish()
    if spread:
        w_finish()
        for k in steps:
            w_done(0, k)
            w_done(1, k)


def per_device(nb, npos, inputs, bn_scale, bn_shift, mid_scale, mid_shift, dilated_weight, w_point, head, targets, assay_slots, assay_counts):
    x = inputs[0]
    nrows, width = x.shape
    cw, _, hid = dilated_weight.shape
    aslot = assay_slots.shape[1]
    nslot = targets.shape[2]
    ntrk = head.shape[0]
    spread = cw % (16 * npos) == 0 and cw % 128 == 0 and npos % (width // hid) == 0
    flat = dilated_weight.reshape(cw, 3 * hid)
    slots = jnp.where(jnp.arange(aslot) < assay_counts[0, 0], assay_slots[0], -1)
    meta = jnp.broadcast_to(slots[:, None], (aslot, 128))
    if spread:
        rest = width // hid
        wide = jnp.swapaxes(w_point.reshape(w_point.shape[0], rest, hid), 0, 1).reshape(cw, hid)
        weights = [jnp.concatenate([flat, wide], axis=1).reshape(npos, cw // npos, 4 * hid)]
        nz = nb
        weight_scratch = [
            pltpu.VMEM((nb, npos, cw // npos, 4 * hid), BF16),
            pltpu.VMEM((hid, width), BF16),
        ]
    else:
        nz = 4
        weights = [
            lax.all_gather(flat, "batch", axis=0, tiled=True).reshape(nz, 1, width // nz, 3 * hid),
            lax.all_gather(w_point, "batch", axis=0, tiled=True),
        ]
        weight_scratch = []
    nchip = npos // 2
    dma = pltpu.SemaphoreType.DMA
    scratch = weight_scratch + [
        pltpu.VMEM((nz, nrows + 2 * STEP, width // nz), BF16),
        pltpu.VMEM((nrows, hid), F32),
        pltpu.VMEM((nrows, hid), BF16),
        pltpu.VMEM((nrows, width), BF16),
        pltpu.VMEM((npos, aslot, width), BF16),
        pltpu.VMEM((nrows, nslot), BF16),
        pltpu.VMEM((nrows, width), BF16),
        pltpu.VMEM((nrows + 2 * STEP, hid), BF16),
        pltpu.VMEM((2, STEP, width), BF16),
        pltpu.VMEM((npos, aslot, width), BF16),
        pltpu.VMEM((nchip, aslot, width), BF16),
        pltpu.VMEM((nchip, aslot, width), BF16),
        pltpu.VMEM((nchip, aslot, width), BF16),
        pltpu.VMEM((nb, aslot, width), BF16),
        pltpu.VMEM((nb, aslot, 128), jnp.int32),
        pltpu.VMEM((nb * aslot, ntrk), BF16),
    ]
    scratch += [dma((4,)), dma((4,)), dma((nb,)), dma((nb,))] + [dma((nchip,))] * 8 + [dma((2, nb)), dma((2, nb))]
    if spread:
        scratch += [dma, dma((2, nb)), dma((2, nb))] + [dma((2, nb, nchip))] * 4
    args = [x, bn_scale[None], bn_shift[None], mid_scale[None], mid_shift[None]] + weights + [head, targets[0], meta]
    vmem = pl.BlockSpec(memory_space=pltpu.VMEM)
    d_in, new_head = pl.pallas_call(
        functools.partial(kernel, nb, npos, spread),
        out_shape=[
            jax.ShapeDtypeStruct((nrows, width), BF16),
            jax.ShapeDtypeStruct((ntrk, width), BF16),
        ],
        in_specs=[vmem] * len(args),
        out_specs=[vmem] * 2,
        scratch_shapes=scratch,
        compiler_params=pltpu.CompilerParams(
            collective_id=0, has_side_effects=True, vmem_limit_bytes=56 * 1024 * 1024
        ),
        cost_estimate=pl.CostEstimate(flops=7_200_000_000, bytes_accessed=13_000_000, transcendentals=4_000_000),
    )(*args)
    return d_in[None], new_head


def solution(mesh):
    in_specs = (
        P("batch", "pos", None),
        P(),
        P(),
        P(),
        P(),
        P("batch", None, None),
        P("batch", None),
        P("pos", None),
        P("batch", "pos", None),
        P("batch", "pos"),
        P("batch", "pos"),
    )
    out_specs = (P("batch", "pos", None), P("pos", None))
    return jax.shard_map(
        functools.partial(per_device, mesh.shape["batch"], mesh.shape["pos"]),
        mesh=mesh,
        in_specs=in_specs,
        out_specs=out_specs,
        check_vma=False,
    )
```

```python
import functools

import jax
import jax.numpy as jnp
from jax import lax
from jax.experimental import pallas as pl
from jax.experimental.pallas import tpu as pltpu
from jax.sharding import PartitionSpec as P

STEP = 32
MESH = pl.DeviceIdType.MESH
F32 = jnp.float32
BF16 = jnp.bfloat16
ROOT = 0.7978845608028654
CUBE = 0.044715


def gelu(v):
    return 0.5 * v * (1.0 + jnp.tanh(ROOT * (v + CUBE * v * v * v)))


def gelu_slope(v):
    sq = v * v
    t = jnp.tanh(ROOT * (v + CUBE * v * sq))
    return 0.5 * (1.0 + t) + 0.5 * v * (1.0 - t * t) * (ROOT * (1.0 + 3.0 * CUBE * sq))


def dot(a, b):
    return jnp.dot(a, b, preferred_element_type=F32)


def dot_t(a, b):
    return lax.dot_general(a, b, (((1,), (1,)), ((), ())), preferred_element_type=F32)


def tdot(a, b):
    return lax.dot_general(a, b, (((0,), (0,)), ((), ())), preferred_element_type=F32)


def kernel(nb, npos, spread, *refs):
    refs = list(refs)
    take = lambda n: [refs.pop(0) for _ in range(n)]
    x_hbm, bsc1, bsh1, msc1, msh1, flat, wpt, head_hbm, goal_hbm, slots, counts = take(11)
    d_in, new_head = take(2)
    if spread:
        w, wp = take(2)
    else:
        w, wp = flat, wpt
    x, head, goal, meta, bsc, bsh, msc, msh, in_sem = take(9)
    acted, hidden, mid, embed, sel, delta, back, dpad, xh = take(9)
    grads, r1buf, part, r2buf, rows_all, meta_all, onehot = take(7)
    (halo_s, halo_r, meta_s, meta_r, sel_s, sel_r, self_s, self_r, r1_s, r1_r, r2_s, r2_r, r3_s, r3_r) = take(14)
    if spread:
        own_sem, w1_s, w1_r, w2_s, w2_r, wf_s, wf_r = take(7)
        rest = wpt.shape[2] // mid.shape[1]
        per = npos // rest

    z = lax.axis_index("batch")
    p = lax.axis_index("pos")
    chip, core = p // 2, p % 2
    nchip = npos // 2
    sib = chip * 2 + (1 - core)
    nrows, width = x.shape
    nz = w.shape[0]
    cw = width // nz
    hid = mid.shape[1]
    nslot = delta.shape[1]
    aslot = sel.shape[1]

    def rc(src, dst, s, r, zz, pp):
        return pltpu.make_async_remote_copy(
            src_ref=src, dst_ref=dst, send_sem=s, recv_sem=r, device_id=(zz, pp), device_id_type=MESH
        )

    def at_chip(d):
        return lax.rem(chip + d, nchip)

    def from_chip(d):
        return lax.rem(chip - d + nchip, nchip)

    loads = []
    if spread:
        hc = mid.shape[1]
        loads.append(pltpu.make_async_copy(flat, w.at[z, :, :, pl.ds(0, 3 * hc)], own_sem.at[0]))
        for q in range(rest):
            src = wpt.at[:, :, pl.ds(q * hc, hc)]
            dst = w.at[z, pl.ds(q * per, per), :, pl.ds(3 * hc, hc)]
            loads.append(pltpu.make_async_copy(src, dst, own_sem.at[1 + q]))
    own = len(loads)
    loads.append(pltpu.make_async_copy(x_hbm, x, in_sem.at[0]))
    loads.append(pltpu.make_async_copy(head_hbm, head, in_sem.at[1]))
    loads.append(pltpu.make_async_copy(goal_hbm, goal, in_sem.at[2]))
    for c in loads:
        c.start()
    for src, dst in ((bsc1, bsc), (bsh1, bsh), (msc1, msc), (msh1, msh)):
        dst[...] = src[...].reshape(dst.shape)
    spot = lax.broadcasted_iota(jnp.int32, (aslot, aslot), 1)
    live = jnp.logical_and(spot == lax.broadcasted_iota(jnp.int32, (aslot, aslot), 0), spot < counts[...])
    column = jnp.sum(jnp.where(live, slots[...] + 1, 0), axis=1, keepdims=True) - 1
    meta[...] = jnp.broadcast_to(column, meta.shape)

    bar = pltpu.get_barrier_semaphore()
    for d in range(1, npos):
        pl.semaphore_signal(bar, inc=1, device_id=(z, lax.rem(p + d, npos)), device_id_type=MESH)
    for d in range(1, nb):
        pl.semaphore_signal(bar, inc=1, device_id=(lax.rem(z + d, nb), p), device_id_type=MESH)
    pl.semaphore_wait(bar, npos - 1 + nb - 1)

    sends = []

    def go(c):
        c.start()
        sends.append(c)

    right, left = lax.rem(p + 1, npos), lax.rem(p + npos - 1, npos)

    def chain(src, dst, ss, rr):
        def copy(di, k, first):
            zz = z - k if di == 0 else z + k
            to = z + 1 if di == 0 else z - 1
            return rc(src if first else dst(zz), dst(zz), ss.at[di, k], rr.at[di, k], to, p)

        def can_send(di, k):
            if di == 0:
                return jnp.logical_and(z + 1 < nb, z - k >= 0)
            return jnp.logical_and(z - 1 >= 0, z + k < nb)

        def start(di, k):
            @pl.when(can_send(di, k))
            def _():
                copy(di, k, k == 0).start()

        def arrive(di, k, body):
            has = (z - k - 1 >= 0) if di == 0 else (z + k + 1 < nb)

            @pl.when(has)
            def _():
                zz = z - k - 1 if di == 0 else z + k + 1
                rc(dst(zz), dst(zz), ss.at[di, k], rr.at[di, k], z, sib).wait_recv()

            if k + 1 < nb - 1:
                start(di, k + 1)
            if body is not None:
                @pl.when(has)
                def _():
                    body(z - k - 1 if di == 0 else z + k + 1)

        def finish():
            for di in (0, 1):
                for k in range(nb - 1):
                    @pl.when(can_send(di, k))
                    def _():
                        copy(di, k, k == 0).wait_send()

        return start, arrive, finish

    if spread:
        gx, gy = lax.rem(chip, 2), chip // 2
        xn, yn = (gy * 2 + 1 - gx) * 2 + core, ((1 - gy) * 2 + gx) * 2 + core
        mine = lax.rem(gx + gy, 2) * 4
        other = 4 - mine
        pair = lambda zz, c: w.at[zz, pl.ds(mine + 2 * c, 2)]
        w_start, w_arrive, w_finish = chain(pair(z, core), lambda zz: pair(zz, core), w1_s, w1_r)
        for c in loads[:own]:
            c.wait()
        w_start(0, 0)
        w_start(1, 0)
    loads[own].wait()
    go(rc(x.at[pl.ds(0, STEP)], xh.at[1], halo_s.at[0], halo_r.at[1], z, left))
    go(rc(x.at[pl.ds(nrows - STEP, STEP)], xh.at[0], halo_s.at[1], halo_r.at[0], z, right))
    for d in range(1, nb):
        go(rc(meta, meta_all.at[z], meta_s.at[d], meta_r.at[d], lax.rem(z + d, nb), p))
    loads[own + 1].wait()

    ntrk = head.shape[0]

    def marks(m):
        return (m[:, 0:1] == lax.broadcasted_iota(jnp.int32, (aslot, ntrk), 1)).astype(BF16)

    sel[p] = dot(marks(meta[...]), head[...]).astype(BF16)
    for d in range(1, nchip):
        go(rc(sel.at[p], sel.at[p], sel_s.at[d], sel_r.at[d], z, at_chip(d) * 2 + core))
    go(rc(sel.at[p], sel.at[p], self_s.at[0], self_r.at[0], z, sib))

    def act_chunk(i):
        cols = pl.ds(i * cw, cw)
        first = x[:, cols].astype(F32) * bsc[:, cols] + bsh[:, cols]
        acted[i, STEP : STEP + nrows] = gelu(first).astype(BF16)

    def w_spread(di, k):
        def body(zz):
            for i, to in enumerate((xn, yn)):
                one = w.at[zz, mine + 2 * core + i]
                rc(one, one, w2_s.at[di, k, i], w2_r.at[di, k, i], z, to).start()
            rc(pair(zz, core), pair(zz, core), wf_s.at[di, k, 2], wf_r.at[di, k, 2], z, sib).start()

        w_arrive(di, k, body)

    def w_shard(di, k):
        zz = z - k - 1 if di == 0 else z + k + 1
        has = (zz >= 0) if di == 0 else (zz < nb)
        return zz, has

    def w_forward(di, k):
        zz, has = w_shard(di, k)

        @pl.when(has)
        def _():
            for i in range(2):
                one = w.at[zz, other + 2 * core + i]
                rc(one, one, w2_s.at[di, k, i], w2_r.at[di, k, i], z, sib).wait_recv()
                rc(one, one, wf_s.at[di, k, i], wf_r.at[di, k, i], z, sib).start()

    def w_ready(di, k):
        zz, has = w_shard(di, k)

        @pl.when(has)
        def _():
            rc(pair(zz, 1 - core), pair(zz, 1 - core), wf_s.at[di, k, 2], wf_r.at[di, k, 2], z, sib).wait_recv()
            for i in range(2):
                one = w.at[zz, other + 2 * (1 - core) + i]
                rc(one, one, wf_s.at[di, k, i], wf_r.at[di, k, i], z, sib).wait_recv()
            conv(zz)

    def w_done(di, k):
        zz, has = w_shard(di, k)

        @pl.when(has)
        def _():
            for i in range(2):
                one = w.at[zz, mine + 2 * core + i]
                rc(one, one, w2_s.at[di, k, i], w2_r.at[di, k, i], z, sib).wait_send()
                one = w.at[zz, other + 2 * core + i]
                rc(one, one, wf_s.at[di, k, i], wf_r.at[di, k, i], z, sib).wait_send()
            rc(pair(zz, core), pair(zz, core), wf_s.at[di, k, 2], wf_r.at[di, k, 2], z, sib).wait_send()

    def wrows(zz, lo, n):
        return w[zz, :, :, lo : lo + n].reshape(cw, n)

    def conv(zz):
        total = hidden[...]
        for k in range(3):
            total = total + dot(acted[zz, k * STEP : k * STEP + nrows], wrows(zz, k * hid, hid))
        hidden[...] = total

    def sel_forward():
        for d in range(1, nchip):
            q = from_chip(d) * 2 + core
            rc(sel.at[q], sel.at[q], sel_s.at[d], sel_r.at[d], z, sib).wait_recv()
            go(rc(sel.at[q], sel.at[q], self_s.at[d], self_r.at[d], z, sib))

    steps = range(nb - 1) if spread else range(0)
    hidden[...] = jnp.zeros_like(hidden)
    for i in range(nz):
        act_chunk(i)
        if i == 0:
            for k in steps[:1]:
                w_spread(0, k)
                w_spread(1, k)
        if i == 2:
            sel_forward()
            for k in steps[:1]:
                w_forward(0, k)
                w_forward(1, k)
    for side, edge in ((0, 0), (1, npos - 1)):
        rc(xh.at[side], xh.at[side], halo_s.at[side], halo_r.at[side], z, sib).wait_recv()
        keep = jnp.where(p == edge, 0.0, 1.0)
        for i in range(nz):
            cols = pl.ds(i * cw, cw)
            first = xh[side, :, cols].astype(F32) * bsc[:, cols] + bsh[:, cols]
            lo = 0 if side == 0 else STEP + nrows
            acted[i, lo : lo + STEP] = (gelu(first) * keep).astype(BF16)
    if spread:
        conv(z)
        for k in steps[1:]:
            w_spread(0, k)
            w_spread(1, k)
            w_ready(0, k - 1)
            w_ready(1, k - 1)
            w_forward(0, k)
            w_forward(1, k)
        for k in steps[-1:]:
            w_ready(0, k)
            w_ready(1, k)
        for zz in range(nb):
            for q in range(rest):
                blk = w[zz, q * per : (q + 1) * per, :, 3 * hid : 4 * hid].reshape(cw // rest, hid)
                wp[zz * (cw // rest) : (zz + 1) * (cw // rest), q * hid : (q + 1) * hid] = blk
    else:
        for i in range(nz):
            conv(i)

    second = hidden[...] * msc[...] + msh[...]
    mid[...] = gelu(second).astype(BF16)
    half = 512
    for n in range(0, width, half):
        embed[:, n : n + half] = (x[:, n : n + half].astype(F32) + dot(mid[...], wp[:, n : n + half])).astype(BF16)

    for d in range(nchip):
        q = from_chip(d) * 2 + 1 - core
        rc(sel.at[q], sel.at[q], self_s.at[d], self_r.at[d], z, sib).wait_recv()

    loads[own + 2].wait()
    group = 256
    per_group = group // aslot
    for j in range(0, nslot, group):
        s = sel[j // aslot : j // aslot + per_group].reshape(group, width)
        pre = dot_t(embed[...], s)
        e = jnp.exp(-jnp.abs(pre))
        soft = jnp.maximum(pre, 0.0) + jnp.log1p(e)
        sig = jnp.where(pre >= 0.0, 1.0, e) / (1.0 + e)
        delta[:, j : j + group] = ((soft - goal[:, j : j + group].astype(F32)) * sig).astype(BF16)
        for n in range(0, width, half):
            g = tdot(delta[:, j : j + group], embed[:, n : n + half]).astype(BF16)
            grads[j // aslot : j // aslot + per_group, :, n : n + half] = g.reshape(per_group, aslot, half)

    order = list(range(1, nchip)) + [0]
    for d in order:
        go(rc(grads.at[at_chip(d) * 2 + 1 - core], r1buf.at[d], r1_s.at[d], r1_r.at[d], z, sib))

    for n in range(0, width, half):
        back[:, n : n + half] = dot(delta[...], sel[:, :, n : n + half].reshape(nslot, half)).astype(BF16)

    for d in order:
        rc(r1buf.at[d], r1buf.at[d], r1_s.at[d], r1_r.at[d], z, sib).wait_recv()
        part[d] = (grads[at_chip(d) * 2 + core].astype(F32) + r1buf[d].astype(F32)).astype(BF16)
        if d:
            go(rc(part.at[d], r2buf.at[d], r2_s.at[d], r2_r.at[d], z, at_chip(d) * 2 + core))

    dmid = dot_t(back[...], wp[...])
    second = hidden[...] * msc[...] + msh[...]
    dpad[STEP : STEP + nrows] = (dmid * gelu_slope(second) * msc[...]).astype(BF16)
    go(rc(dpad.at[pl.ds(STEP, STEP)], dpad.at[pl.ds(STEP + nrows, STEP)], halo_s.at[2], halo_r.at[3], z, left))
    go(rc(dpad.at[pl.ds(nrows, STEP)], dpad.at[pl.ds(0, STEP)], halo_s.at[3], halo_r.at[2], z, right))

    total = part[0].astype(F32)
    for d in range(1, nchip):
        rc(r2buf.at[d], r2buf.at[d], r2_s.at[d], r2_r.at[d], z, sib).wait_recv()
        total = total + r2buf[d].astype(F32)
    rows_all[z] = total.astype(BF16)
    g_start, g_arrive, g_finish = chain(rows_all.at[z], lambda zz: rows_all.at[zz], r3_s, r3_r)
    g_start(0, 0)
    g_start(1, 0)

    for side, edge, lo in ((0, 0, 0), (1, npos - 1, STEP + nrows)):
        rc(dpad.at[pl.ds(lo, STEP)], dpad.at[pl.ds(lo, STEP)], halo_s.at[2], halo_r.at[2 + side], z, sib).wait_recv()

        @pl.when(p == edge)
        def _():
            dpad[lo : lo + STEP] = jnp.zeros((STEP, hid), BF16)

    arrivals = list(range(nb - 1))
    for i in range(nz):
        cols = pl.ds(i * cw, cw)
        dact = dot_t(dpad[2 * STEP : 2 * STEP + nrows], wrows(i, 0, hid))
        dact = dact + dot_t(dpad[STEP : STEP + nrows], wrows(i, hid, hid))
        dact = dact + dot_t(dpad[0:nrows], wrows(i, 2 * hid, hid))
        first = x[:, cols].astype(F32) * bsc[:, cols] + bsh[:, cols]
        d_in[:, cols] = (back[:, cols].astype(F32) + dact * gelu_slope(first) * bsc[:, cols]).astype(BF16)
        if i < nz - 1 and arrivals:
            k = arrivals.pop(0)
            g_arrive(0, k, None)
            g_arrive(1, k, None)
    for k in arrivals:
        g_arrive(0, k, None)
        g_arrive(1, k, None)

    for d in range(1, nb):
        zz = lax.rem(z - d + nb, nb)
        rc(meta_all.at[zz], meta_all.at[zz], meta_s.at[d], meta_r.at[d], z, sib).wait_recv()
    meta_all[z] = meta[...]
    for zz in range(nb):
        onehot[zz * aslot : (zz + 1) * aslot] = marks(meta_all[zz])
    for n in range(0, width, half):
        d_head = tdot(onehot[...], rows_all[:, :, n : n + half].reshape(nb * aslot, half))
        new_head[:, n : n + half] = (head[:, n : n + half].astype(F32) - 0.004 * d_head).astype(BF16)

    for c in sends:
        c.wait_send()
    g_finish()
    if spread:
        w_finish()
        for k in steps:
            w_done(0, k)
            w_done(1, k)


def per_device(nb, npos, inputs, bn_scale, bn_shift, mid_scale, mid_shift, dilated_weight, w_point, head, targets, assay_slots, assay_counts):
    x = inputs[0]
    nrows, width = x.shape
    cw, _, hid = dilated_weight.shape
    aslot = assay_slots.shape[1]
    nslot = targets.shape[2]
    ntrk = head.shape[0]
    rest = width // hid
    spread = npos == 8 and cw % (16 * npos) == 0 and cw % 128 == 0 and npos % rest == 0
    flat = dilated_weight.reshape(cw, 3 * hid)
    if spread:
        slab = cw // npos
        weights = [flat.reshape(npos, slab, 3 * hid), w_point.reshape(npos // rest, slab, width)]
        nz = nb
        weight_scratch = [pltpu.VMEM((nb, npos, slab, 4 * hid), BF16), pltpu.VMEM((hid, width), BF16)]
    else:
        nz = 4
        weights = [
            lax.all_gather(flat, "batch", axis=0, tiled=True).reshape(nz, 1, width // nz, 3 * hid),
            lax.all_gather(w_point, "batch", axis=0, tiled=True),
        ]
        weight_scratch = []
    nchip = npos // 2
    dma = pltpu.SemaphoreType.DMA
    scratch = weight_scratch + [
        pltpu.VMEM((nrows, width), BF16),
        pltpu.VMEM((ntrk, width), BF16),
        pltpu.VMEM((nrows, nslot), BF16),
        pltpu.VMEM((aslot, 128), jnp.int32),
        pltpu.VMEM((1, width), F32),
        pltpu.VMEM((1, width), F32),
        pltpu.VMEM((1, hid), F32),
        pltpu.VMEM((1, hid), F32),
        dma((3,)),
        pltpu.VMEM((nz, nrows + 2 * STEP, width // nz), BF16),
        pltpu.VMEM((nrows, hid), F32),
        pltpu.VMEM((nrows, hid), BF16),
        pltpu.VMEM((nrows, width), BF16),
        pltpu.VMEM((npos, aslot, width), BF16),
        pltpu.VMEM((nrows, nslot), BF16),
        pltpu.VMEM((nrows, width), BF16),
        pltpu.VMEM((nrows + 2 * STEP, hid), BF16),
        pltpu.VMEM((2, STEP, width), BF16),
        pltpu.VMEM((npos, aslot, width), BF16),
        pltpu.VMEM((nchip, aslot, width), BF16),
        pltpu.VMEM((nchip, aslot, width), BF16),
        pltpu.VMEM((nchip, aslot, width), BF16),
        pltpu.VMEM((nb, aslot, width), BF16),
        pltpu.VMEM((nb, aslot, 128), jnp.int32),
        pltpu.VMEM((nb * aslot, ntrk), BF16),
    ]
    scratch += [dma((4,)), dma((4,)), dma((nb,)), dma((nb,))] + [dma((nchip,))] * 8 + [dma((2, nb)), dma((2, nb))]
    if spread:
        scratch += [dma((1 + rest,)), dma((2, nb)), dma((2, nb))] + [dma((2, nb, 2))] * 2 + [dma((2, nb, 3))] * 2
    args = [x, bn_scale, bn_shift, mid_scale, mid_shift] + weights + [head, targets[0], assay_slots, assay_counts]
    vmem = pl.BlockSpec(memory_space=pltpu.VMEM)
    far = pl.BlockSpec(memory_space=pl.ANY)
    d_in, new_head = pl.pallas_call(
        functools.partial(kernel, nb, npos, spread),
        out_shape=[
            jax.ShapeDtypeStruct((nrows, width), BF16),
            jax.ShapeDtypeStruct((ntrk, width), BF16),
        ],
        in_specs=[far] + [vmem] * 4 + ([far] * 2 if spread else [vmem] * 2) + [far] * 2 + [vmem] * 2,
        out_specs=[vmem] * 2,
        scratch_shapes=scratch,
        compiler_params=pltpu.CompilerParams(
            collective_id=0, has_side_effects=True, vmem_limit_bytes=56 * 1024 * 1024
        ),
        cost_estimate=pl.CostEstimate(flops=7_200_000_000, bytes_accessed=13_000_000, transcendentals=4_000_000),
    )(*args)
    return d_in[None], new_head


def solution(mesh):
    in_specs = (
        P("batch", "pos", None),
        P(),
        P(),
        P(),
        P(),
        P("batch", None, None),
        P("batch", None),
        P("pos", None),
        P("batch", "pos", None),
        P("batch", "pos"),
        P("batch", "pos"),
    )
    out_specs = (P("batch", "pos", None), P("pos", None))
    return jax.shard_map(
        functools.partial(per_device, mesh.shape["batch"], mesh.shape["pos"]),
        mesh=mesh,
        in_specs=in_specs,
        out_specs=out_specs,
        check_vma=False,
    )
```

```python
import functools

import jax
import jax.numpy as jnp
from jax import lax
from jax.experimental import pallas as pl
from jax.experimental.pallas import tpu as pltpu
from jax.sharding import PartitionSpec as P

STEP = 32
MESH = pl.DeviceIdType.MESH
F32 = jnp.float32
BF16 = jnp.bfloat16
ROOT = 0.7978845608028654
CUBE = 0.044715


def gelu(v):
    return 0.5 * v * (1.0 + jnp.tanh(ROOT * (v + CUBE * v * v * v)))


def gelu_slope(v):
    sq = v * v
    t = jnp.tanh(ROOT * (v + CUBE * v * sq))
    return 0.5 * (1.0 + t) + 0.5 * v * (1.0 - t * t) * (ROOT * (1.0 + 3.0 * CUBE * sq))


def dot(a, b):
    return jnp.dot(a, b, preferred_element_type=F32)


def dot_t(a, b):
    return lax.dot_general(a, b, (((1,), (1,)), ((), ())), preferred_element_type=F32)


def tdot(a, b):
    return lax.dot_general(a, b, (((0,), (0,)), ((), ())), preferred_element_type=F32)


def kernel(nb, npos, spread, *refs):
    refs = list(refs)
    take = lambda n: [refs.pop(0) for _ in range(n)]
    x_hbm, bsc1, bsh1, msc1, msh1, flat, wpt, head_hbm, goal_hbm, slots, counts = take(11)
    d_in, new_head = take(2)
    if spread:
        w, wp = take(2)
    else:
        w, wp = flat, wpt
    x, head, goal, meta, bsc, bsh, msc, msh, in_sem = take(9)
    acted, hidden, mid, embed, sel, delta, back, dpad, xh = take(9)
    grads, r1buf, part, r2buf, rows_all, meta_all, onehot = take(7)
    (halo_s, halo_r, meta_s, meta_r, sel_s, sel_r, self_s, self_r, r1_s, r1_r, r2_s, r2_r, r3_s, r3_r) = take(14)
    if spread:
        own_sem, w1_s, w1_r, w2_s, w2_r, wf_s, wf_r = take(7)
        rest = wpt.shape[2] // mid.shape[1]
        per = npos // rest

    z = lax.axis_index("batch")
    p = lax.axis_index("pos")
    chip, core = p // 2, p % 2
    nchip = npos // 2
    sib = chip * 2 + (1 - core)
    nrows, width = x.shape
    nz = w.shape[0]
    cw = width // nz
    hid = mid.shape[1]
    nslot = delta.shape[1]
    aslot = sel.shape[1]

    def rc(src, dst, s, r, zz, pp):
        return pltpu.make_async_remote_copy(
            src_ref=src, dst_ref=dst, send_sem=s, recv_sem=r, device_id=(zz, pp), device_id_type=MESH
        )

    def at_chip(d):
        return lax.rem(chip + d, nchip)

    def from_chip(d):
        return lax.rem(chip - d + nchip, nchip)

    loads = []
    if spread:
        hc = mid.shape[1]
        for k in range(3):
            loads.append(pltpu.make_async_copy(flat.at[k], w.at[z, :, :, pl.ds(k * hc, hc)], own_sem.at[rest + k]))
        for q in range(rest):
            src = wpt.at[:, :, pl.ds(q * hc, hc)]
            dst = w.at[z, pl.ds(q * per, per), :, pl.ds(3 * hc, hc)]
            loads.append(pltpu.make_async_copy(src, dst, own_sem.at[q]))
    own = len(loads)
    loads.append(pltpu.make_async_copy(x_hbm, x, in_sem.at[0]))
    loads.append(pltpu.make_async_copy(head_hbm, head, in_sem.at[1]))
    loads.append(pltpu.make_async_copy(goal_hbm, goal, in_sem.at[2]))
    for c in loads:
        c.start()
    for src, dst in ((bsc1, bsc), (bsh1, bsh), (msc1, msc), (msh1, msh)):
        dst[...] = src[...].reshape(dst.shape)
    spot = lax.broadcasted_iota(jnp.int32, (aslot, aslot), 1)
    live = jnp.logical_and(spot == lax.broadcasted_iota(jnp.int32, (aslot, aslot), 0), spot < counts[...])
    column = jnp.sum(jnp.where(live, slots[...] + 1, 0), axis=1, keepdims=True) - 1
    meta[...] = jnp.broadcast_to(column, meta.shape)

    bar = pltpu.get_barrier_semaphore()
    for d in range(1, npos):
        pl.semaphore_signal(bar, inc=1, device_id=(z, lax.rem(p + d, npos)), device_id_type=MESH)
    for d in range(1, nb):
        pl.semaphore_signal(bar, inc=1, device_id=(lax.rem(z + d, nb), p), device_id_type=MESH)
    pl.semaphore_wait(bar, npos - 1 + nb - 1)

    sends = []

    def go(c):
        c.start()
        sends.append(c)

    right, left = lax.rem(p + 1, npos), lax.rem(p + npos - 1, npos)

    def chain(src, dst, ss, rr):
        def copy(di, k, first):
            zz = z - k if di == 0 else z + k
            to = z + 1 if di == 0 else z - 1
            return rc(src if first else dst(zz), dst(zz), ss.at[di, k], rr.at[di, k], to, p)

        def can_send(di, k):
            if di == 0:
                return jnp.logical_and(z + 1 < nb, z - k >= 0)
            return jnp.logical_and(z - 1 >= 0, z + k < nb)

        def start(di, k):
            @pl.when(can_send(di, k))
            def _():
                copy(di, k, k == 0).start()

        def arrive(di, k, body):
            has = (z - k - 1 >= 0) if di == 0 else (z + k + 1 < nb)

            @pl.when(has)
            def _():
                zz = z - k - 1 if di == 0 else z + k + 1
                rc(dst(zz), dst(zz), ss.at[di, k], rr.at[di, k], z, sib).wait_recv()

            if k + 1 < nb - 1:
                start(di, k + 1)
            if body is not None:
                @pl.when(has)
                def _():
                    body(z - k - 1 if di == 0 else z + k + 1)

        def finish():
            for di in (0, 1):
                for k in range(nb - 1):
                    @pl.when(can_send(di, k))
                    def _():
                        copy(di, k, k == 0).wait_send()

        return start, arrive, finish

    if spread:
        gx, gy = lax.rem(chip, 2), chip // 2
        xn, yn = (gy * 2 + 1 - gx) * 2 + core, ((1 - gy) * 2 + gx) * 2 + core
        mine = lax.rem(gx + gy, 2) * 4
        other = 4 - mine
        pair = lambda zz, c: w.at[zz, pl.ds(mine + 2 * c, 2)]
        w_start, w_arrive, w_finish = chain(pair(z, core), lambda zz: pair(zz, core), w1_s, w1_r)
        for c in loads[:own]:
            c.wait()
        w_start(0, 0)
        w_start(1, 0)
    loads[own].wait()
    go(rc(x.at[pl.ds(0, STEP)], xh.at[1], halo_s.at[0], halo_r.at[1], z, left))
    go(rc(x.at[pl.ds(nrows - STEP, STEP)], xh.at[0], halo_s.at[1], halo_r.at[0], z, right))
    for d in range(1, nb):
        go(rc(meta, meta_all.at[z], meta_s.at[d], meta_r.at[d], lax.rem(z + d, nb), p))
    loads[own + 1].wait()

    ntrk = head.shape[0]

    def marks(m):
        return (m[:, 0:1] == lax.broadcasted_iota(jnp.int32, (aslot, ntrk), 1)).astype(BF16)

    sel[p] = dot(marks(meta[...]), head[...]).astype(BF16)
    for d in range(1, nchip):
        go(rc(sel.at[p], sel.at[p], sel_s.at[d], sel_r.at[d], z, at_chip(d) * 2 + core))
    go(rc(sel.at[p], sel.at[p], self_s.at[0], self_r.at[0], z, sib))

    def act_chunk(i):
        cols = pl.ds(i * cw, cw)
        first = x[:, cols].astype(F32) * bsc[:, cols] + bsh[:, cols]
        acted[i, STEP : STEP + nrows] = gelu(first).astype(BF16)

    def w_spread(di, k):
        def body(zz):
            for i, to in enumerate((xn, yn)):
                one = w.at[zz, mine + 2 * core + i]
                rc(one, one, w2_s.at[di, k, i], w2_r.at[di, k, i], z, to).start()
            rc(pair(zz, core), pair(zz, core), wf_s.at[di, k, 2], wf_r.at[di, k, 2], z, sib).start()

        w_arrive(di, k, body)

    def w_shard(di, k):
        zz = z - k - 1 if di == 0 else z + k + 1
        has = (zz >= 0) if di == 0 else (zz < nb)
        return zz, has

    def w_forward(di, k):
        zz, has = w_shard(di, k)

        @pl.when(has)
        def _():
            for i in range(2):
                one = w.at[zz, other + 2 * core + i]
                rc(one, one, w2_s.at[di, k, i], w2_r.at[di, k, i], z, sib).wait_recv()
                rc(one, one, wf_s.at[di, k, i], wf_r.at[di, k, i], z, sib).start()

    def w_ready(di, k):
        zz, has = w_shard(di, k)

        @pl.when(has)
        def _():
            rc(pair(zz, 1 - core), pair(zz, 1 - core), wf_s.at[di, k, 2], wf_r.at[di, k, 2], z, sib).wait_recv()
            for i in range(2):
                one = w.at[zz, other + 2 * (1 - core) + i]
                rc(one, one, wf_s.at[di, k, i], wf_r.at[di, k, i], z, sib).wait_recv()
            conv(zz)

    def w_done(di, k):
        zz, has = w_shard(di, k)

        @pl.when(has)
        def _():
            for i in range(2):
                one = w.at[zz, mine + 2 * core + i]
                rc(one, one, w2_s.at[di, k, i], w2_r.at[di, k, i], z, sib).wait_send()
                one = w.at[zz, other + 2 * core + i]
                rc(one, one, wf_s.at[di, k, i], wf_r.at[di, k, i], z, sib).wait_send()
            rc(pair(zz, core), pair(zz, core), wf_s.at[di, k, 2], wf_r.at[di, k, 2], z, sib).wait_send()

    def wrows(zz, lo, n):
        return w[zz, :, :, lo : lo + n].reshape(cw, n)

    def conv(zz):
        total = hidden[...]
        for k in range(3):
            total = total + dot(acted[zz, k * STEP : k * STEP + nrows], wrows(zz, k * hid, hid))
        hidden[...] = total

    def sel_forward():
        for d in range(1, nchip):
            q = from_chip(d) * 2 + core
            rc(sel.at[q], sel.at[q], sel_s.at[d], sel_r.at[d], z, sib).wait_recv()
            go(rc(sel.at[q], sel.at[q], self_s.at[d], self_r.at[d], z, sib))

    steps = range(nb - 1) if spread else range(0)
    hidden[...] = jnp.zeros_like(hidden)
    for i in range(nz):
        act_chunk(i)
        if i == 0:
            for k in steps[:1]:
                w_spread(0, k)
                w_spread(1, k)
        if i == 2:
            sel_forward()
            for k in steps[:1]:
                w_forward(0, k)
                w_forward(1, k)
    for side, edge in ((0, 0), (1, npos - 1)):
        rc(xh.at[side], xh.at[side], halo_s.at[side], halo_r.at[side], z, sib).wait_recv()
        keep = jnp.where(p == edge, 0.0, 1.0)
        for i in range(nz):
            cols = pl.ds(i * cw, cw)
            first = xh[side, :, cols].astype(F32) * bsc[:, cols] + bsh[:, cols]
            lo = 0 if side == 0 else STEP + nrows
            acted[i, lo : lo + STEP] = (gelu(first) * keep).astype(BF16)
    if spread:
        conv(z)
        for k in steps[1:]:
            w_spread(0, k)
            w_spread(1, k)
            w_ready(0, k - 1)
            w_ready(1, k - 1)
            w_forward(0, k)
            w_forward(1, k)
        for k in steps[-1:]:
            w_ready(0, k)
            w_ready(1, k)
        for zz in range(nb):
            for q in range(rest):
                blk = w[zz, q * per : (q + 1) * per, :, 3 * hid : 4 * hid].reshape(cw // rest, hid)
                wp[zz * (cw // rest) : (zz + 1) * (cw // rest), q * hid : (q + 1) * hid] = blk
    else:
        for i in range(nz):
            conv(i)

    second = hidden[...] * msc[...] + msh[...]
    mid[...] = gelu(second).astype(BF16)
    half = 512
    for n in range(0, width, half):
        embed[:, n : n + half] = (x[:, n : n + half].astype(F32) + dot(mid[...], wp[:, n : n + half])).astype(BF16)

    for d in range(nchip):
        q = from_chip(d) * 2 + 1 - core
        rc(sel.at[q], sel.at[q], self_s.at[d], self_r.at[d], z, sib).wait_recv()

    loads[own + 2].wait()
    group = 256
    per_group = group // aslot
    for j in range(0, nslot, group):
        s = sel[j // aslot : j // aslot + per_group].reshape(group, width)
        pre = dot_t(embed[...], s)
        e = jnp.exp(-jnp.abs(pre))
        soft = jnp.maximum(pre, 0.0) + jnp.log1p(e)
        sig = jnp.where(pre >= 0.0, 1.0, e) / (1.0 + e)
        delta[:, j : j + group] = ((soft - goal[:, j : j + group].astype(F32)) * sig).astype(BF16)
        for n in range(0, width, half):
            g = tdot(delta[:, j : j + group], embed[:, n : n + half]).astype(BF16)
            grads[j // aslot : j // aslot + per_group, :, n : n + half] = g.reshape(per_group, aslot, half)

    order = list(range(1, nchip)) + [0]
    for d in order:
        go(rc(grads.at[at_chip(d) * 2 + 1 - core], r1buf.at[d], r1_s.at[d], r1_r.at[d], z, sib))

    for n in range(0, width, half):
        back[:, n : n + half] = dot(delta[...], sel[:, :, n : n + half].reshape(nslot, half)).astype(BF16)

    for d in order:
        rc(r1buf.at[d], r1buf.at[d], r1_s.at[d], r1_r.at[d], z, sib).wait_recv()
        part[d] = (grads[at_chip(d) * 2 + core].astype(F32) + r1buf[d].astype(F32)).astype(BF16)
        if d:
            go(rc(part.at[d], r2buf.at[d], r2_s.at[d], r2_r.at[d], z, at_chip(d) * 2 + core))

    dmid = dot_t(back[...], wp[...])
    second = hidden[...] * msc[...] + msh[...]
    dpad[STEP : STEP + nrows] = (dmid * gelu_slope(second) * msc[...]).astype(BF16)
    go(rc(dpad.at[pl.ds(STEP, STEP)], dpad.at[pl.ds(STEP + nrows, STEP)], halo_s.at[2], halo_r.at[3], z, left))
    go(rc(dpad.at[pl.ds(nrows, STEP)], dpad.at[pl.ds(0, STEP)], halo_s.at[3], halo_r.at[2], z, right))

    total = part[0].astype(F32)
    for d in range(1, nchip):
        rc(r2buf.at[d], r2buf.at[d], r2_s.at[d], r2_r.at[d], z, sib).wait_recv()
        total = total + r2buf[d].astype(F32)
    rows_all[z] = total.astype(BF16)
    g_start, g_arrive, g_finish = chain(rows_all.at[z], lambda zz: rows_all.at[zz], r3_s, r3_r)
    g_start(0, 0)
    g_start(1, 0)

    for side, edge, lo in ((0, 0, 0), (1, npos - 1, STEP + nrows)):
        rc(dpad.at[pl.ds(lo, STEP)], dpad.at[pl.ds(lo, STEP)], halo_s.at[2], halo_r.at[2 + side], z, sib).wait_recv()

        @pl.when(p == edge)
        def _():
            dpad[lo : lo + STEP] = jnp.zeros((STEP, hid), BF16)

    arrivals = list(range(nb - 1))
    for i in range(nz):
        cols = pl.ds(i * cw, cw)
        dact = dot_t(dpad[2 * STEP : 2 * STEP + nrows], wrows(i, 0, hid))
        dact = dact + dot_t(dpad[STEP : STEP + nrows], wrows(i, hid, hid))
        dact = dact + dot_t(dpad[0:nrows], wrows(i, 2 * hid, hid))
        first = x[:, cols].astype(F32) * bsc[:, cols] + bsh[:, cols]
        d_in[:, cols] = (back[:, cols].astype(F32) + dact * gelu_slope(first) * bsc[:, cols]).astype(BF16)
        if i < nz - 1 and arrivals:
            k = arrivals.pop(0)
            g_arrive(0, k, None)
            g_arrive(1, k, None)
    for k in arrivals:
        g_arrive(0, k, None)
        g_arrive(1, k, None)

    for d in range(1, nb):
        zz = lax.rem(z - d + nb, nb)
        rc(meta_all.at[zz], meta_all.at[zz], meta_s.at[d], meta_r.at[d], z, sib).wait_recv()
    meta_all[z] = meta[...]
    for zz in range(nb):
        onehot[zz * aslot : (zz + 1) * aslot] = marks(meta_all[zz])
    for n in range(0, width, half):
        d_head = tdot(onehot[...], rows_all[:, :, n : n + half].reshape(nb * aslot, half))
        new_head[:, n : n + half] = (head[:, n : n + half].astype(F32) - 0.004 * d_head).astype(BF16)

    for c in sends:
        c.wait_send()
    g_finish()
    if spread:
        w_finish()
        for k in steps:
            w_done(0, k)
            w_done(1, k)


def per_device(nb, npos, inputs, bn_scale, bn_shift, mid_scale, mid_shift, dilated_weight, w_point, head, targets, assay_slots, assay_counts):
    x = inputs[0]
    nrows, width = x.shape
    cw, _, hid = dilated_weight.shape
    aslot = assay_slots.shape[1]
    nslot = targets.shape[2]
    ntrk = head.shape[0]
    rest = width // hid
    spread = npos == 8 and cw % (16 * npos) == 0 and cw % 128 == 0 and npos % rest == 0
    flat = dilated_weight.reshape(cw, 3 * hid)
    if spread:
        slab = cw // npos
        weights = [jnp.swapaxes(dilated_weight, 0, 1).reshape(3, npos, slab, hid), w_point.reshape(npos // rest, slab, width)]
        nz = nb
        weight_scratch = [pltpu.VMEM((nb, npos, slab, 4 * hid), BF16), pltpu.VMEM((hid, width), BF16)]
    else:
        nz = 4
        weights = [
            lax.all_gather(flat, "batch", axis=0, tiled=True).reshape(nz, 1, width // nz, 3 * hid),
            lax.all_gather(w_point, "batch", axis=0, tiled=True),
        ]
        weight_scratch = []
    nchip = npos // 2
    dma = pltpu.SemaphoreType.DMA
    scratch = weight_scratch + [
        pltpu.VMEM((nrows, width), BF16),
        pltpu.VMEM((ntrk, width), BF16),
        pltpu.VMEM((nrows, nslot), BF16),
        pltpu.VMEM((aslot, 128), jnp.int32),
        pltpu.VMEM((1, width), F32),
        pltpu.VMEM((1, width), F32),
        pltpu.VMEM((1, hid), F32),
        pltpu.VMEM((1, hid), F32),
        dma((3,)),
        pltpu.VMEM((nz, nrows + 2 * STEP, width // nz), BF16),
        pltpu.VMEM((nrows, hid), F32),
        pltpu.VMEM((nrows, hid), BF16),
        pltpu.VMEM((nrows, width), BF16),
        pltpu.VMEM((npos, aslot, width), BF16),
        pltpu.VMEM((nrows, nslot), BF16),
        pltpu.VMEM((nrows, width), BF16),
        pltpu.VMEM((nrows + 2 * STEP, hid), BF16),
        pltpu.VMEM((2, STEP, width), BF16),
        pltpu.VMEM((npos, aslot, width), BF16),
        pltpu.VMEM((nchip, aslot, width), BF16),
        pltpu.VMEM((nchip, aslot, width), BF16),
        pltpu.VMEM((nchip, aslot, width), BF16),
        pltpu.VMEM((nb, aslot, width), BF16),
        pltpu.VMEM((nb, aslot, 128), jnp.int32),
        pltpu.VMEM((nb * aslot, ntrk), BF16),
    ]
    scratch += [dma((4,)), dma((4,)), dma((nb,)), dma((nb,))] + [dma((nchip,))] * 8 + [dma((2, nb)), dma((2, nb))]
    if spread:
        scratch += [dma((3 + rest,)), dma((2, nb)), dma((2, nb))] + [dma((2, nb, 2))] * 2 + [dma((2, nb, 3))] * 2
    args = [x, bn_scale, bn_shift, mid_scale, mid_shift] + weights + [head, targets[0], assay_slots, assay_counts]
    vmem = pl.BlockSpec(memory_space=pltpu.VMEM)
    far = pl.BlockSpec(memory_space=pl.ANY)
    d_in, new_head = pl.pallas_call(
        functools.partial(kernel, nb, npos, spread),
        out_shape=[
            jax.ShapeDtypeStruct((nrows, width), BF16),
            jax.ShapeDtypeStruct((ntrk, width), BF16),
        ],
        in_specs=[far] + [vmem] * 4 + ([far] * 2 if spread else [vmem] * 2) + [far] * 2 + [vmem] * 2,
        out_specs=[vmem] * 2,
        scratch_shapes=scratch,
        compiler_params=pltpu.CompilerParams(
            collective_id=0, has_side_effects=True, vmem_limit_bytes=56 * 1024 * 1024
        ),
        cost_estimate=pl.CostEstimate(flops=7_200_000_000, bytes_accessed=13_000_000, transcendentals=4_000_000),
    )(*args)
    return d_in[None], new_head


def solution(mesh):
    in_specs = (
        P("batch", "pos", None),
        P(),
        P(),
        P(),
        P(),
        P("batch", None, None),
        P("batch", None),
        P("pos", None),
        P("batch", "pos", None),
        P("batch", "pos"),
        P("batch", "pos"),
    )
    out_specs = (P("batch", "pos", None), P("pos", None))
    return jax.shard_map(
        functools.partial(per_device, mesh.shape["batch"], mesh.shape["pos"]),
        mesh=mesh,
        in_specs=in_specs,
        out_specs=out_specs,
        check_vma=False,
    )
```
